1024 devices in a mesh: rows: 256 (over z, x, core), cols: 4 (over y).
Axes of the slice: x: 4, y: 4, z: 32, core: 2. Of those that a mesh axis runs over, the one named last changes fastest.
Arguments:
- a_vals: bfloat16 [8192, 64, 512], P(('rows', 'cols')), may hold values from -0.25 to 0.25
- a_cols: int32 [8192, 8], P('rows'), may hold values from 0 to 8191, as said below
- p_vals: bfloat16 [8192, 64, 256], P('rows'), may hold values from -1.5 to 1.5
- p_cols: int32 [8192, 4], replicated, may hold values from 0 to 1023, as said below
- colpos: int32 [1024], replicated, may hold values from 0 to 3, as said below
Outputs:
- coarse_matrix: float32 [1024, 64, 768], P('rows', None, 'cols')
The draws below stay inside these ranges and needn't reach their ends.
Inputs may be any that keep to these rules, and one draw needn't show every extreme that they name: a_cols[i, 0] = i, and every entry j of row i satisfies |j - i| <= 4. `p_cols`: the 4 entries of a row are distinct. The first is the row's aggregate, in the row's partition; each coarse block is the first entry of exactly 8 rows. The others lie in the row's partition, or also in partition i // 32 - 1 when i % 32 < 4, or in partition i // 32 + 1 when i % 32 >= 28. `colpos`: over each partition's 4 coarse blocks, a permutation of 0 to 3.
All inputs are finite; a program needn't handle non-finite values.
Results may differ from the reference program's by a relative error of at most 0.0029.
Values may be sent and summed in bfloat16 or wider, within the bound.
No kernel may reach another device: no remote copies, remote signals or barrier semaphores. Data moves between devices by JAX's collectives and lax.ppermute only.
A program may use at most 64 MiB of HBM per device.

```python
import jax
import jax.numpy as jnp
from jax import lax

B = 64
KA = 8
KP = 4
HB = 4
CBC = 1
FB = 32
CB = 4
NF = 8192
NC = 1024
N_ROWS = 256
N_COLS = 4


def draw_a_cols(key, part):
    key = jax.random.fold_in(key, 1)
    span = 2 * HB
    row_ids = jnp.arange(NF, dtype=jnp.int32)[:, None]
    scores = jax.random.randint(key, (NF, span), 0, 1 << 20) * span + jnp.arange(span, dtype=jnp.int32)[None, :]
    order = jnp.argsort(scores, axis=1)[:, :KA - 1].astype(jnp.int32)
    offsets = jnp.where(order < HB, order - HB, order - HB + 1)
    columns = row_ids + offsets
    columns = jnp.where(columns < 0, -columns, columns)
    columns = jnp.where(columns >= NF, 2 * (NF - 1) - columns, columns)
    return jnp.concatenate([row_ids, columns], axis=1).astype(jnp.int32)


def draw_p_cols(key, part):
    key = jax.random.fold_in(key, 2)
    home_key, pick_key = jax.random.split(key)
    partitions = NF // FB
    row_ids = jnp.arange(NF, dtype=jnp.int32)
    part_of = row_ids // FB
    local_row = row_ids % FB
    home_scores = jax.random.randint(home_key, (partitions, FB), 0, 1 << 20) * FB + jnp.arange(FB, dtype=jnp.int32)[None, :]
    shuffled = jnp.argsort(home_scores, axis=1).astype(jnp.int32)
    home_local = (shuffled % CB).reshape(NF)
    slot_ids = jnp.arange(3 * CB, dtype=jnp.int32)[None, :]
    side = slot_ids // CB
    lower_ok = (local_row < HB) & (part_of > 0)
    upper_ok = (local_row >= FB - HB) & (part_of < partitions - 1)
    allowed = (side == 1) | (side == 0) & lower_ok[:, None] | (side == 2) & upper_ok[:, None]
    allowed = allowed & (slot_ids != CB + home_local[:, None])
    pick_scores = jax.random.randint(pick_key, (NF, 3 * CB), 1, 1 << 20)
    pick_scores = jnp.where(allowed, pick_scores, 0) * (3 * CB) + slot_ids
    chosen = lax.top_k(pick_scores, KP - 1)[1].astype(jnp.int32)
    others = (part_of[:, None] - 1) * CB + chosen
    home = part_of * CB + home_local
    return jnp.concatenate([home[:, None], others], axis=1).astype(jnp.int32)


def draw_colpos(key, part):
    key = jax.random.fold_in(key, 3)
    partitions = NC // CB
    scores = jax.random.randint(key, (partitions, CB), 0, 1 << 20) * CB + jnp.arange(CB, dtype=jnp.int32)[None, :]
    return jnp.argsort(scores, axis=1).astype(jnp.int32).reshape(NC)


def steps_of(stream_key, extent, shards, least, largest):
    loudness, own = 1.0, jax.random.fold_in(stream_key, 6)
    for axis_at, parts in shards:
        steps = jnp.exp(jax.random.uniform(jax.random.fold_in(own, axis_at), (parts,), jnp.float32, least / len(shards), largest / len(shards)))
        loudness = loudness * jnp.repeat(steps, extent[axis_at] // parts).reshape([-1 if axis == axis_at else 1 for axis in range(len(extent))])
    return loudness


def normal_values(rng, extent, deviation, most, cuts=(), held_as=jnp.bfloat16):
    factor_of = steps_of(rng, extent, cuts, -0.22, 0.18) if cuts else 1.0
    drawn = jax.random.normal(rng, extent, jnp.float32) * deviation * factor_of
    return jnp.minimum(jnp.maximum(drawn, -most), most).astype(held_as)


def setup_inputs(seed: int = 0) -> dict:
    splits = jax.random.split(jax.random.key(seed), 6)
    return {
        "a_vals": normal_values(splits[0], (NF, B, KA * B), (KA * B) ** -0.5, 0.25, ((0, 1024),)),
        "a_cols": draw_a_cols(jax.random.fold_in(splits[5], 71), 0),
        "p_vals": normal_values(splits[2], (NF, B, KP * B), 0.25, 1.5, ((0, 256),)),
        "p_cols": draw_p_cols(jax.random.fold_in(splits[5], 71), 0),
        "colpos": draw_colpos(jax.random.fold_in(splits[5], 71), 0),
    }


def reference(a_vals, a_cols, p_vals, p_cols, colpos):
    highest = lax.Precision.HIGHEST
    win_blocks = 3 * CB
    ext_rows = FB + 2 * HB
    padded_p = jnp.pad(p_vals, ((HB, HB), (0, 0), (0, 0)))
    padded_cols = jnp.pad(p_cols, ((HB, HB), (0, 0)))
    padded_pos = jnp.pad(colpos, (CB, CB))

    def one_part(part_idx):
        part_idx = part_idx.astype(jnp.int32)
        ext_p = lax.dynamic_slice_in_dim(padded_p, part_idx * FB, ext_rows, 0).astype(jnp.float32)
        ext_cols = lax.dynamic_slice_in_dim(padded_cols, part_idx * FB, ext_rows, 0)
        win_pos = lax.dynamic_slice_in_dim(padded_pos, part_idx * CB, win_blocks, 0)
        relative = ext_cols - (part_idx - 1) * CB
        matches = relative[:, :, None] == jnp.arange(win_blocks, dtype=jnp.int32)[None, None, :]
        col_slot = jnp.sum(jnp.where(matches, win_pos[None, None, :], 0), axis=2)
        band_index = relative // CB
        slots = jnp.where(jnp.any(matches, axis=2), (col_slot // CBC) * 3 * CBC + band_index * CBC + col_slot % CBC, -1)
        picker = (slots[:, :, None] == jnp.arange(win_blocks, dtype=jnp.int32)[None, None, :]).astype(jnp.float32)
        dense_p = jnp.einsum("jmw,jbme->jbwe", picker, ext_p.reshape(ext_rows, B, KP, B), precision=highest)
        dense_p = dense_p.reshape(ext_rows, B, win_blocks * B)
        rows_a = lax.dynamic_slice_in_dim(a_vals, part_idx * FB, FB, 0).astype(jnp.float32)
        local_idx = lax.dynamic_slice_in_dim(a_cols, part_idx * FB, FB, 0) - (part_idx * FB - HB)
        accum = jnp.zeros((FB, B, win_blocks * B), jnp.float32)
        for term in range(KA):
            accum = accum + jnp.einsum("ibe,iew->ibw", rows_a[:, :, term * B:(term + 1) * B], dense_p[local_idx[:, term]], precision=highest)
        ap_rows = lax.optimization_barrier(accum.astype(jnp.bfloat16)).astype(jnp.float32)
        own_p = ext_p[HB:HB + FB]
        products = jnp.einsum("ibl,ibw->ilw", own_p, ap_rows, precision=highest)
        own_rel = (ext_cols[HB:HB + FB] - (part_idx - 1) * CB).reshape(FB * KP)
        targets = (jnp.arange(win_blocks, dtype=jnp.int32)[:, None] == own_rel[None, :]).astype(jnp.float32)
        summed = jnp.dot(targets, products.reshape(FB * KP, B * win_blocks * B), precision=highest)
        return summed.reshape(win_blocks, B, win_blocks * B)

    terms = lax.map(one_part, jnp.arange(N_ROWS, dtype=jnp.int32))
    grid_terms = terms.reshape(N_ROWS, 3 * CB, B, N_COLS, 3, CBC * B)
    middle = grid_terms[:, CB:2 * CB]
    zero_band = jnp.zeros((N_ROWS, CB, B, N_COLS, 1, CBC * B), jnp.float32)
    zero_part = jnp.zeros((1, CB, B, N_COLS, 3, CBC * B), jnp.float32)
    upper = grid_terms[:, 2 * CB:]
    upper_moved = jnp.concatenate([upper[:, :, :, :, 1:], zero_band], axis=4)
    from_left = jnp.concatenate([zero_part, upper_moved[:-1]], axis=0)
    lower = grid_terms[:, :CB]
    lower_moved = jnp.concatenate([zero_band, lower[:, :, :, :, :2]], axis=4)
    from_right = jnp.concatenate([lower_moved[1:], zero_part], axis=0)
    summed_all = middle + from_left + from_right
    return summed_all.reshape(NC, B, N_COLS * 3 * CBC * B)
```

```python
import jax
import jax.numpy as jnp
from jax import lax
from jax.experimental import pallas as pl
from jax.experimental.pallas import tpu as pltpu
from jax.sharding import PartitionSpec as P

B = 64
KA = 8
KP = 4
HB = 4
LANES = 2 * B
VMEM = pl.BlockSpec(memory_space=pltpu.VMEM)
SMEM = pl.BlockSpec(memory_space=pltpu.SMEM)


def spread_row(x, slot_ref, base, groups, left):
    x = x.astype(jnp.float32)
    pieces = []
    for v in range(KP // 2):
        pair = x[:, v * LANES : (v + 1) * LANES]
        turned = pltpu.roll(pair, B, 1)
        pieces.append((pair, turned, slot_ref[base + 2 * v], slot_ref[base + 2 * v + 1]))
    out = []
    for c in range(groups):
        total = None
        for pair, turned, s0, s1 in pieces:
            def flag(s, w):
                return (s == w).astype(jnp.float32)
            keep = jnp.where(left, flag(s0, 2 * c), flag(s1, 2 * c + 1))
            swap = jnp.where(left, flag(s1, 2 * c), flag(s0, 2 * c + 1))
            term = pair * keep + turned * swap
            total = term if total is None else total + term
        out.append(total.astype(jnp.bfloat16))
    return out


def terms_kernel(slot_ref, idx_ref, g_ref, a_ref, p_ref, halo_ref, own_ref, edge_ref, pd_ref, ap_ref):
    groups = own_ref.shape[0]
    count = a_ref.shape[0]
    fine = p_ref.shape[0]
    g = g_ref[0]
    lower = g < groups // 2
    left = lax.broadcasted_iota(jnp.int32, (1, LANES), 1) < B
    for j in range(count + 2 * HB):
        row = jnp.clip(count * g - HB + j, 0, fine - 1)
        x = p_ref[row]
        if j < HB:
            x = jnp.where(g == 0, halo_ref[j], x)
        if j >= count + HB:
            x = jnp.where(g == groups - 1, halo_ref[j - count - HB], x)
        for c, block in enumerate(spread_row(x, slot_ref, j * KP, groups, left)):
            pd_ref[j * B : (j + 1) * B, c * LANES : (c + 1) * LANES] = block
    for i in range(count):
        picked = jnp.concatenate(
            [pd_ref[pl.ds(pl.multiple_of(idx_ref[i * KA + k] * B, B), B), :] for k in range(KA)], axis=0
        )
        ap = jnp.dot(a_ref[i], picked, preferred_element_type=jnp.float32)
        ap_ref[i * B : (i + 1) * B, :] = ap.astype(jnp.bfloat16)
    own_p = pd_ref[HB * B : (HB + count) * B, :]
    terms = lax.dot_general(
        own_p, ap_ref[...], (((0,), (0,)), ((), ())), preferred_element_type=jnp.float32
    )
    for row in range(groups):
        first = terms[2 * row * B : (2 * row + 1) * B]
        second = terms[(2 * row + 1) * B : (2 * row + 2) * B]
        own = jnp.where(lower, second, first)
        edge = jnp.where(lower, first, second).astype(jnp.bfloat16)
        for c in range(groups):
            own_ref[c, row * B : (row + 1) * B, :] = own[:, c * LANES : (c + 1) * LANES]
            edge_ref[c, row * B : (row + 1) * B, :] = edge[:, c * LANES : (c + 1) * LANES]


def final_kernel(pos_ref, got_ref, out_ref, low_ref, high_ref):
    groups = got_ref.shape[0]
    half = groups // 2
    low = got_ref[0].astype(jnp.float32)
    high = got_ref[half].astype(jnp.float32)
    for g in range(1, half):
        low += got_ref[g].astype(jnp.float32)
        high += got_ref[half + g].astype(jnp.float32)
    low_ref[...] = low
    high_ref[...] = high
    left = lax.broadcasted_iota(jnp.int32, (1, LANES), 1) < B
    for h in range(out_ref.shape[0]):
        rows = pl.ds(pl.multiple_of(pos_ref[h] * B, B), B)
        high = high_ref[rows, :]
        out_ref[h, :, :LANES] = low_ref[rows, :] + jnp.where(left, 0.0, pltpu.roll(high, B, 1))
        out_ref[h, :, LANES:] = high[:, B:]


def on_device(a_vals, a_cols, p_vals, p_cols, colpos):
    groups = lax.axis_size("cols")
    parts = lax.axis_size("rows")
    g = lax.axis_index("cols")
    p = lax.axis_index("rows")
    count = a_vals.shape[0]
    fine = p_vals.shape[0]
    coarse = groups
    near = count + 2 * HB
    last = groups - 1

    edge_p = lax.dynamic_slice_in_dim(p_vals, jnp.where(g == 0, fine - HB, 0), HB, 0)
    inward = [(q * groups, (q + 1) * groups) for q in range(parts - 1)]
    inward += [((q + 1) * groups + last, q * groups + last) for q in range(parts - 1)]
    halo_p = lax.ppermute(edge_p, ("rows", "cols"), inward)

    start = p * fine + g * count
    near_cols = lax.dynamic_slice_in_dim(jnp.pad(p_cols, ((HB, HB), (0, 0))), start, near, 0)
    win_pos = lax.dynamic_slice_in_dim(jnp.pad(colpos, (coarse, coarse)), p * coarse, 3 * coarse, 0)
    relative = near_cols - (p - 1) * coarse
    match = relative[:, :, None] == jnp.arange(3 * coarse, dtype=jnp.int32)
    place = 2 * win_pos + jnp.arange(3 * coarse, dtype=jnp.int32) // coarse
    first_band = jnp.where(g < groups // 2, 0, 1)
    slots = jnp.sum(jnp.where(match, place - first_band, 0), axis=2).reshape(-1)
    own_cols = lax.dynamic_slice_in_dim(a_cols, g * count, count, 0)
    local = (own_cols - (start - HB)).reshape(-1)

    shape = (groups, coarse * B, LANES)
    own, edge = pl.pallas_call(
        terms_kernel,
        out_shape=(
            jax.ShapeDtypeStruct(shape, jnp.float32),
            jax.ShapeDtypeStruct(shape, jnp.bfloat16),
        ),
        in_specs=[SMEM, SMEM, SMEM, VMEM, VMEM, VMEM],
        out_specs=(VMEM, VMEM),
        scratch_shapes=[
            pltpu.VMEM((near * B, groups * LANES), jnp.bfloat16),
            pltpu.VMEM((count * B, groups * LANES), jnp.bfloat16),
        ],
        compiler_params=pltpu.CompilerParams(vmem_limit_bytes=32 << 20),
        name="terms",
    )(slots, local, jnp.reshape(g, (1,)), a_vals, p_vals, halo_p)

    across = [(q * groups, (q - 1) * groups + last) for q in range(1, parts)]
    across += [(target, source) for source, target in across]
    taken = lax.ppermute(edge, ("rows", "cols"), across)
    sent = (own + taken.astype(jnp.float32)).astype(jnp.bfloat16)
    got = lax.all_to_all(sent, "cols", 0, 0)

    return pl.pallas_call(
        final_kernel,
        out_shape=jax.ShapeDtypeStruct((coarse, B, 3 * B), jnp.float32),
        in_specs=[SMEM, VMEM],
        out_specs=VMEM,
        scratch_shapes=[pltpu.VMEM((coarse * B, LANES), jnp.float32)] * 2,
        name="final",
    )(win_pos[coarse : 2 * coarse], got)


def solution(mesh):
    placed = (P(("rows", "cols"), None, None), P("rows", None), P("rows", None, None), P(), P())
    return jax.shard_map(
        on_device, mesh=mesh, in_specs=placed, out_specs=P("rows", None, "cols"), check_vma=False
    )
```

```python
import jax
import jax.numpy as jnp
from jax import lax
from jax.experimental import pallas as pl
from jax.experimental.pallas import tpu as pltpu
from jax.sharding import PartitionSpec as P

B = 64
KA = 8
KP = 4
HB = 4
LANES = 2 * B
VMEM = pl.BlockSpec(memory_space=pltpu.VMEM)
SMEM = pl.BlockSpec(memory_space=pltpu.SMEM)


def spread_row(x, slot_ref, base, groups, left):
    x = x.astype(jnp.float32)
    pieces = []
    for v in range(KP // 2):
        pair = x[:, v * LANES : (v + 1) * LANES]
        turned = pltpu.roll(pair, B, 1)
        pieces.append((pair, turned, slot_ref[base + 2 * v], slot_ref[base + 2 * v + 1]))
    out = []
    for c in range(groups):
        total = None
        for pair, turned, s0, s1 in pieces:
            def flag(s, w):
                return (s == w).astype(jnp.float32)
            keep = jnp.where(left, flag(s0, 2 * c), flag(s1, 2 * c + 1))
            swap = jnp.where(left, flag(s1, 2 * c), flag(s0, 2 * c + 1))
            term = pair * keep + turned * swap
            total = term if total is None else total + term
        out.append(total.astype(jnp.bfloat16))
    return out


def spread_rows(load, slot_ref, pd_ref, first, count, groups, left, below=0):
    for t in range(count):
        row = first + t
        for c, block in enumerate(spread_row(load(t), slot_ref, row * KP, groups, left)):
            rows = pl.ds(pl.multiple_of((row - below) * B, B), B)
            pd_ref[rows, c * LANES : (c + 1) * LANES] = block


def ap_row(a, idx_ref, base, pd_ref, below=0):
    picked = jnp.concatenate(
        [pd_ref[pl.ds(pl.multiple_of((idx_ref[base + k] - below) * B, B), B), :] for k in range(KA)], axis=0
    )
    return jnp.dot(a, picked, preferred_element_type=jnp.float32).astype(jnp.bfloat16)


def left_half():
    return lax.broadcasted_iota(jnp.int32, (1, LANES), 1) < B


def own_kernel(slot_ref, idx_ref, g_ref, a_ref, p_ref, pd_ref, ap_ref):
    groups = pd_ref.shape[1] // LANES
    count = a_ref.shape[0]
    fine = p_ref.shape[0]
    g = g_ref[0]

    def load(t):
        return p_ref[jnp.clip(count * g - HB + t, 0, fine - 1)]

    spread_rows(load, slot_ref, pd_ref, HB, count + 2 * HB, groups, left_half(), HB)
    for i in range(count):
        ap_ref[i * B : (i + 1) * B, :] = ap_row(a_ref[i], idx_ref, i * KA, pd_ref, HB)


def edge_kernel(
    slot_ref, idx_ref, far_ref, g_ref, pos_ref, a_ref, far_a_ref, far_p_ref, own_pd_ref, own_ap_ref,
    sent_ref, pd_ref, ap_ref,
):
    groups = sent_ref.shape[0]
    count = a_ref.shape[0]
    g = g_ref[0]
    lower = g < groups // 2
    low_edge = g == 0
    pd_ref[HB * B : (count + 3 * HB) * B, :] = own_pd_ref[...]
    ap_ref[HB * B : (count + HB) * B, :] = own_ap_ref[...]

    @pl.when(jnp.logical_or(low_edge, g == groups - 1))
    def _():
        first = jnp.where(low_edge, 0, count + 2 * HB)
        spread_rows(lambda t: far_p_ref[t], slot_ref, pd_ref, first, 2 * HB, groups, left_half())
        own = jnp.where(low_edge, 0, count - HB)
        far = jnp.where(low_edge, 0, count + HB)
        for t in range(HB):
            rows = pl.ds(pl.multiple_of((HB + own + t) * B, B), B)
            ap_ref[rows, :] = ap_row(a_ref[own + t], idx_ref, (own + t) * KA, pd_ref)
            rows = pl.ds(pl.multiple_of((far + t) * B, B), B)
            ap_ref[rows, :] = ap_row(far_a_ref[t * B : (t + 1) * B, :], far_ref, t * KA, pd_ref)

    @pl.when(jnp.logical_and(g > 0, g < groups - 1))
    def _():
        zeros = jnp.zeros((HB * B, groups * LANES), jnp.bfloat16)
        ap_ref[0 : HB * B, :] = zeros
        ap_ref[(count + HB) * B :, :] = zeros

    first = jnp.where(lower, 0, HB)
    size = (count + HB) * B
    terms = lax.dot_general(
        pd_ref[pl.ds(pl.multiple_of((HB + first) * B, B), size), :],
        ap_ref[pl.ds(pl.multiple_of(first * B, B), size), :],
        (((0,), (0,)), ((), ())),
        preferred_element_type=jnp.float32,
    )
    for place in range(groups):
        one = terms[2 * place * B : (2 * place + 1) * B]
        two = terms[(2 * place + 1) * B : (2 * place + 2) * B]
        own = jnp.where(lower, two, one).astype(jnp.bfloat16)
        h = jnp.int32(0)
        for other in range(1, groups):
            h += jnp.where(pos_ref[other] == place, other, 0)
        rows = pl.ds(pl.multiple_of(h * B, B), B)
        for c in range(groups):
            sent_ref[c, rows, :] = own[:, c * LANES : (c + 1) * LANES]


def on_device(a_vals, a_cols, p_vals, p_cols, colpos):
    groups = lax.axis_size("cols")
    parts = lax.axis_size("rows")
    g = lax.axis_index("cols")
    p = lax.axis_index("rows")
    count = a_vals.shape[0]
    fine = p_vals.shape[0]
    coarse = groups
    last = groups - 1
    table = count + 4 * HB
    start = p * fine + g * count

    sent_p = lax.dynamic_slice_in_dim(p_vals, jnp.where(g < groups // 2, fine - 2 * HB, 0), 2 * HB, 0)
    pairs = [(q * groups + 1, (q + 1) * groups) for q in range(parts - 1)]
    pairs += [((q + 1) * groups + last - 1, q * groups + last) for q in range(parts - 1)]
    far_p = lax.ppermute(sent_p, ("rows", "cols"), pairs)

    own_cols = lax.dynamic_slice_in_dim(a_cols, g * count, count, 0)
    edge_row = jnp.where(g == 0, 0, count - HB)
    edge_a = lax.dynamic_slice_in_dim(a_vals, edge_row, HB, 0).reshape(HB * B, KA * B)
    steps = lax.dynamic_slice_in_dim(own_cols, edge_row, HB, 0) + HB
    steps = steps - (start + edge_row + jnp.arange(HB, dtype=jnp.int32))[:, None]
    steps = steps.reshape(1, HB * KA).astype(jnp.bfloat16)
    steps = jnp.pad(steps, ((0, 15), (0, KA * B - HB * KA)))
    pairs = [(q * groups, (q - 1) * groups + last) for q in range(1, parts)]
    pairs += [(target, source) for source, target in pairs]
    far_a = lax.ppermute(jnp.concatenate([edge_a, steps], axis=0), ("rows", "cols"), pairs)

    pad = 2 * HB
    near_cols = lax.dynamic_slice_in_dim(jnp.pad(p_cols, ((pad, pad), (0, 0))), start, table, 0)
    win_pos = lax.dynamic_slice_in_dim(jnp.pad(colpos, (coarse, coarse)), p * coarse, 3 * coarse, 0)
    relative = near_cols - (p - 1) * coarse
    match = relative[:, :, None] == jnp.arange(3 * coarse, dtype=jnp.int32)
    place = 2 * win_pos + jnp.arange(3 * coarse, dtype=jnp.int32) // coarse
    first_band = jnp.where(g < groups // 2, 0, 1)
    slots = jnp.sum(jnp.where(match, place - first_band, 0), axis=2).reshape(-1)
    local = (own_cols - (start - pad)).reshape(-1)
    own_pos = win_pos[coarse : 2 * coarse]
    which = jnp.reshape(g, (1,))

    pd, ap = pl.pallas_call(
        own_kernel,
        out_shape=(
            jax.ShapeDtypeStruct(((count + 2 * HB) * B, groups * LANES), jnp.bfloat16),
            jax.ShapeDtypeStruct((count * B, groups * LANES), jnp.bfloat16),
        ),
        in_specs=[SMEM, SMEM, SMEM, VMEM, VMEM],
        out_specs=(VMEM, VMEM),
        compiler_params=pltpu.CompilerParams(vmem_limit_bytes=24 << 20),
        cost_estimate=pl.CostEstimate(flops=1 << 31, bytes_accessed=4 << 20, transcendentals=0),
        name="own_rows",
    )(slots, local, which, a_vals, p_vals)

    far_steps = far_a[HB * B, : HB * KA].astype(jnp.int32)
    far_steps = far_steps + jnp.arange(HB * KA, dtype=jnp.int32) // KA
    far_local = far_steps + jnp.where(g == 0, 0, count + HB)
    sent = pl.pallas_call(
        edge_kernel,
        out_shape=jax.ShapeDtypeStruct((groups, coarse * B, LANES), jnp.bfloat16),
        in_specs=[SMEM] * 5 + [VMEM] * 5,
        out_specs=VMEM,
        scratch_shapes=[
            pltpu.VMEM((table * B, groups * LANES), jnp.bfloat16),
            pltpu.VMEM(((count + 2 * HB) * B, groups * LANES), jnp.bfloat16),
        ],
        compiler_params=pltpu.CompilerParams(vmem_limit_bytes=24 << 20),
        name="edge_rows",
    )(slots, local, far_local, which, own_pos, a_vals, far_a, far_p, pd, ap)

    got = lax.all_to_all(sent, "cols", 0, 0).astype(jnp.float32)
    half = groups // 2
    low = sum(got[c] for c in range(1, half)) + got[0]
    high = sum(got[c] for c in range(half + 1, groups)) + got[half]
    out = jnp.pad(low, ((0, 0), (0, B))) + jnp.pad(high, ((0, 0), (B, 0)))
    return out.reshape(coarse, B, 3 * B)


def solution(mesh):
    placed = (P(("rows", "cols"), None, None), P("rows", None), P("rows", None, None), P(), P())
    return jax.shard_map(
        on_device, mesh=mesh, in_specs=placed, out_specs=P("rows", None, "cols"), check_vma=False
    )
```

```python
import jax
import jax.numpy as jnp
from jax import lax
from jax.experimental import pallas as pl
from jax.experimental.pallas import tpu as pltpu
from jax.sharding import PartitionSpec as P

B = 64
KA = 8
KP = 4
HB = 4
LANES = 2 * B
TILE = 16
VMEM = pl.BlockSpec(memory_space=pltpu.VMEM)
SMEM = pl.BlockSpec(memory_space=pltpu.SMEM)


def block(i):
    return pl.ds(pl.multiple_of(i * B, B), B)


def edge_of(g, p):
    lower = jnp.logical_and(g == 0, p > 0)
    upper = jnp.logical_and(g == lax.axis_size("cols") - 1, p < lax.axis_size("rows") - 1)
    return jnp.logical_or(lower, upper)


def turned_pairs(x):
    x = x.astype(jnp.float32)
    pairs = [x[:, v * LANES : (v + 1) * LANES] for v in range(KP // 2)]
    return [(pair, pltpu.roll(pair, B, 1)) for pair in pairs]


def spread(pairs, slots, pieces, ref, row):
    left = lax.broadcasted_iota(jnp.int32, (1, LANES), 1) < B
    side = jnp.where(left, 0, 1)
    keeps = [jnp.where(left, slots[2 * v], slots[2 * v + 1]) - side for v in range(len(pairs))]
    swaps = [jnp.where(left, slots[2 * v + 1], slots[2 * v]) - side for v in range(len(pairs))]
    for c in range(pieces):
        total = jnp.zeros((B, LANES), jnp.float32)
        for (pair, turned), keep, swap in zip(pairs, keeps, swaps):
            total = jnp.where(keep == 2 * c, pair, jnp.where(swap == 2 * c, turned, total))
        ref[block(row), c * LANES : (c + 1) * LANES] = total.astype(jnp.bfloat16)


def ap_row(a, indices, pd_ref):
    picked = jnp.concatenate([pd_ref[block(i), :] for i in indices], axis=0)
    return jnp.dot(a, picked, preferred_element_type=jnp.float32).astype(jnp.bfloat16)


def transposed_dot(x, y):
    return lax.dot_general(x, y, (((0,), (0,)), ((), ())), preferred_element_type=jnp.float32)


def pack_kernel(at_ref, a_ref, _, msg_ref):
    g, p = lax.axis_index("cols"), lax.axis_index("rows")
    fine = at_ref.shape[1]
    tiles = HB * B // TILE
    first = jnp.where(g == 0, 0, a_ref.shape[0] - tiles)
    msg_ref[:tiles] = a_ref[pl.ds(first, tiles)]
    rows = p * fine + lax.broadcasted_iota(jnp.int32, (KA, fine), 1)
    steps = (at_ref[...] - rows + HB).astype(jnp.float32)
    steps = jnp.concatenate([steps, jnp.zeros((KA, LANES - fine), jnp.float32)], axis=1)
    steps = jnp.concatenate([steps, jnp.zeros((TILE - KA, LANES), jnp.float32)], axis=0)
    msg_ref[tiles] = jnp.zeros((TILE, KA * B), jnp.bfloat16)
    msg_ref[tiles, :, :LANES] = steps.astype(jnp.bfloat16)


def own_kernel(
    at_ref, pos_ref, cols_ref, a_ref, p_ref, pd_ref, pn_ref, part_ref, ints_ref, ap_buf
):
    g, p = lax.axis_index("cols"), lax.axis_index("rows")
    groups = lax.axis_size("cols")
    coarse = groups
    count = a_ref.shape[0]
    fine = p_ref.shape[0]
    near = count + 2 * HB
    start = p * fine + g * count

    edge = edge_of(g, p)
    low = g == 0
    base = 1 - p - jnp.where(g < groups // 2, 0, 1)

    def columns(f):
        return [cols_ref[m, f + 2 * HB] for m in range(KP)]

    def slots_of(cols):
        return [2 * pos_ref[h] + lax.div(h, coarse) + base for h in cols]

    for t in range(2 * HB):
        cols = columns(jnp.where(low, t - 2 * HB, count + t))
        for m, (slot, h) in enumerate(zip(slots_of(cols), cols)):
            ints_ref[t * KP + m] = slot
            ints_ref[(2 * HB + t) * KP + m] = h - p * coarse
    for t in range(HB):
        lane = g * count + jnp.where(low, t, count - HB + t)
        shift = start - jnp.where(low, 2 * HB, 0)
        for k in range(KA):
            ints_ref[4 * HB * KP + t * KA + k] = at_ref[k, lane] - shift

    for j in range(near):
        pairs = turned_pairs(p_ref[jnp.clip(count * g - HB + j, 0, fine - 1)])
        cols = columns(j - HB)
        spread(pairs, slots_of(cols), groups, pd_ref, j)
        if HB <= j < HB + count:
            spread(pairs, [h - p * coarse for h in cols], coarse // 2, pn_ref, j - HB)

    first = jnp.where(jnp.logical_and(edge, low), HB, 0)

    def own_row(t, i):
        picks = [at_ref[k, g * count + i] - (start - HB) for k in range(KA)]
        ap_buf[t * B : (t + 1) * B, :] = ap_row(a_ref[i], picks, pd_ref)

    for t in range(count - HB):
        own_row(t, first + t)

    @pl.when(edge)
    def _():
        size = (count - HB) * B
        rows = pl.ds(pl.multiple_of(first * B, B), size)
        part_ref[...] = transposed_dot(pn_ref[rows, :], ap_buf[:size, :])

    @pl.when(jnp.logical_not(edge))
    def _():
        for t in range(count - HB, count):
            own_row(t, t)
        part_ref[...] = transposed_dot(pn_ref[...], ap_buf[...])


def edge_kernel(
    ints_ref, far_ref, own_a_ref, far_a_ref, far_p_ref, pd_ref, pn_ref, part_ref,
    sent_ref, table, lhs, ap_buf,
):
    g, p = lax.axis_index("cols"), lax.axis_index("rows")
    groups = lax.axis_size("cols")
    edge = edge_of(g, p)
    low = g == 0
    size = HB * B
    tiles = size // TILE
    count = pn_ref.shape[0] // B
    fine = far_ref.shape[1]

    def store(total):
        for c in range(groups):
            sent_ref[c] = total[:, c * LANES : (c + 1) * LANES].astype(jnp.bfloat16)

    def half(second):
        return pl.ds(pl.multiple_of(jnp.where(second, size, 0), size), size)

    @pl.when(edge)
    def _():
        rows = pl.ds(pl.multiple_of(jnp.where(low, 2 * size, 0), size), 2 * size)
        table[rows, :] = pd_ref[size : 3 * size, :]
        lhs[half(low), :] = pn_ref[pl.ds(pl.multiple_of(jnp.where(low, 0, (count - HB) * B), B), size), :]
        shift = jnp.where(low, 0, 2 * HB)
        for t in range(2 * HB):
            slots = [ints_ref[t * KP + m] for m in range(KP)]
            spread(turned_pairs(far_p_ref[t]), slots, groups, table, shift + t)
        for t in range(HB):
            s = jnp.where(low, HB, 0) + t
            slots = [ints_ref[(2 * HB + s) * KP + m] for m in range(KP)]
            spread(turned_pairs(far_p_ref[s]), slots, groups // 2, lhs, jnp.where(low, t, HB + t))
        each = B // TILE
        for t in range(HB):
            a = own_a_ref[t * each : (t + 1) * each].reshape(B, KA * B)
            picks = [ints_ref[4 * HB * KP + t * KA + k] for k in range(KA)]
            ap_buf[block(jnp.where(low, HB + t, t)), :] = ap_row(a, picks, table)
        for t in range(HB):
            a = far_a_ref[t * each : (t + 1) * each].reshape(B, KA * B)
            lane = jnp.where(low, fine - HB, 0) + t
            picks = [far_ref[k, lane] + jnp.where(low, t, HB + t) for k in range(KA)]
            ap_buf[block(jnp.where(low, t, HB + t)), :] = ap_row(a, picks, table)
        store(part_ref[...] + transposed_dot(lhs[...], ap_buf[...]))

    @pl.when(jnp.logical_not(edge))
    def _():
        store(part_ref[...])


def on_device(a_vals, a_cols, p_vals, p_cols, colpos):
    groups = lax.axis_size("cols")
    parts = lax.axis_size("rows")
    count = a_vals.shape[0]
    fine = p_vals.shape[0]
    coarse = groups
    g = lax.axis_index("cols")
    p = lax.axis_index("rows")
    last = groups - 1
    near = count + 2 * HB
    wide = groups * LANES
    tiles = HB * B // TILE
    bf16, f32, i32 = jnp.bfloat16, jnp.float32, jnp.int32
    params = pltpu.CompilerParams(vmem_limit_bytes=16 << 20)
    at = a_cols.T

    msg_p = lax.dynamic_slice_in_dim(p_vals, jnp.where(g < groups // 2, fine - 2 * HB, 0), 2 * HB, 0)
    pairs = [(q * groups + 1, (q + 1) * groups) for q in range(parts - 1)]
    pairs += [((q + 1) * groups + last - 1, q * groups + last) for q in range(parts - 1)]
    far_p = lax.ppermute(msg_p, ("rows", "cols"), pairs)
    msg_a = pl.pallas_call(
        pack_kernel,
        out_shape=jax.ShapeDtypeStruct((tiles + 1, TILE, KA * B), bf16),
        in_specs=[VMEM, VMEM, pl.BlockSpec(memory_space=pl.ANY)],
        out_specs=VMEM,
        compiler_params=params,
        name="pack",
    )(at, a_vals.reshape(count * B // TILE, TILE, KA * B), msg_p)
    pairs = [(q * groups, (q - 1) * groups + last) for q in range(1, parts)]
    pairs += [(target, source) for source, target in pairs]
    far_a = lax.ppermute(msg_a, ("rows", "cols"), pairs)

    pad = 2 * HB
    padded = jnp.pad(p_cols.T, ((0, 0), (pad, pad)))
    near_cols = lax.dynamic_slice_in_dim(padded, p * fine + g * count, count + 2 * pad, 1)
    pd, pn, part, ints = pl.pallas_call(
        own_kernel,
        out_shape=(
            jax.ShapeDtypeStruct((near * B, wide), bf16),
            jax.ShapeDtypeStruct((count * B, coarse * B), bf16),
            jax.ShapeDtypeStruct((coarse * B, wide), f32),
            jax.ShapeDtypeStruct((LANES,), i32),
        ),
        in_specs=[SMEM, SMEM, SMEM, VMEM, VMEM],
        out_specs=(VMEM, VMEM, VMEM, SMEM),
        scratch_shapes=[pltpu.VMEM((count * B, wide), bf16)],
        compiler_params=params,
        cost_estimate=pl.CostEstimate(flops=1 << 31, bytes_accessed=4 << 20, transcendentals=0),
        name="own_rows",
    )(at, colpos, near_cols, a_vals, p_vals)

    far_steps = far_a[tiles, :KA, :fine].astype(i32)
    sent = pl.pallas_call(
        edge_kernel,
        out_shape=jax.ShapeDtypeStruct((groups, coarse * B, LANES), bf16),
        in_specs=[SMEM] * 2 + [VMEM] * 6,
        out_specs=VMEM,
        scratch_shapes=[
            pltpu.VMEM((near * B, wide), bf16),
            pltpu.VMEM((2 * HB * B, coarse * B), bf16),
            pltpu.VMEM((2 * HB * B, wide), bf16),
        ],
        compiler_params=params,
        name="edge_rows",
    )(ints, far_steps, msg_a, far_a, far_p, pd, pn, part)

    got = lax.all_to_all(sent, "cols", 0, 0).astype(f32)
    half = groups // 2
    low = sum(got[c] for c in range(1, half)) + got[0]
    high = sum(got[c] for c in range(half + 1, groups)) + got[half]
    out = jnp.pad(low, ((0, 0), (0, B))) + jnp.pad(high, ((0, 0), (B, 0)))
    return out.reshape(coarse, B, 3 * B)


def solution(mesh):
    placed = (P(("rows", "cols"), None, None), P("rows", None), P("rows", None, None), P(), P())
    return jax.shard_map(
        on_device, mesh=mesh, in_specs=placed, out_specs=P("rows", None, "cols"), check_vma=False
    )
```

```python
import jax
import jax.numpy as jnp
from jax import lax
from jax.experimental import pallas as pl
from jax.experimental.pallas import tpu as pltpu
from jax.sharding import PartitionSpec as P

B = 64
KA = 8
KP = 4
HB = 4
LANES = 2 * B
VMEM = pl.BlockSpec(memory_space=pltpu.VMEM)
SMEM = pl.BlockSpec(memory_space=pltpu.SMEM)


def block(i):
    return pl.ds(pl.multiple_of(i * B, B), B)


def edge_of(g, p):
    lower = jnp.logical_and(g == 0, p > 0)
    upper = jnp.logical_and(g == lax.axis_size("cols") - 1, p < lax.axis_size("rows") - 1)
    return jnp.logical_or(lower, upper)


def turned_pairs(x):
    x = x.astype(jnp.float32)
    pairs = [x[:, v * LANES : (v + 1) * LANES] for v in range(KP // 2)]
    return [(pair, pltpu.roll(pair, B, 1)) for pair in pairs]


def spread(pairs, slots, pieces, ref, row):
    left = lax.broadcasted_iota(jnp.int32, (1, LANES), 1) < B
    side = jnp.where(left, 0, 1)
    keeps = [jnp.where(left, slots[2 * v], slots[2 * v + 1]) - side for v in range(len(pairs))]
    swaps = [jnp.where(left, slots[2 * v + 1], slots[2 * v]) - side for v in range(len(pairs))]
    for c in range(pieces):
        total = jnp.zeros((B, LANES), jnp.float32)
        for (pair, turned), keep, swap in zip(pairs, keeps, swaps):
            total = jnp.where(keep == 2 * c, pair, jnp.where(swap == 2 * c, turned, total))
        ref[block(row), c * LANES : (c + 1) * LANES] = total.astype(jnp.bfloat16)


def ap_row(a, indices, pd_ref):
    picked = jnp.concatenate([pd_ref[block(i), :] for i in indices], axis=0)
    return jnp.dot(a, picked, preferred_element_type=jnp.float32).astype(jnp.bfloat16)


def transposed_dot(x, y):
    return lax.dot_general(x, y, (((0,), (0,)), ((), ())), preferred_element_type=jnp.float32)


def pack_kernel(a_ref, _, msg_ref):
    first = jnp.where(lax.axis_index("cols") == 0, 0, a_ref.shape[0] - HB)
    msg_ref[...] = a_ref[pl.ds(first, HB)]


def lookups(pos_ref, cols_ref):
    g, p = lax.axis_index("cols"), lax.axis_index("rows")
    coarse = groups = lax.axis_size("cols")
    base = 1 - p - jnp.where(g < groups // 2, 0, 1)

    def columns(f):
        return [cols_ref[m, f + 2 * HB] for m in range(KP)]

    def slots_of(cols):
        return [2 * pos_ref[h] + lax.div(h, coarse) + base for h in cols]

    def inner(cols):
        return [h - p * coarse for h in cols]

    return columns, slots_of, inner


def own_kernel(at_ref, pos_ref, cols_ref, a_ref, p_ref, pd_ref, pn_ref, part_ref, ap_ref):
    g, p = lax.axis_index("cols"), lax.axis_index("rows")
    groups = lax.axis_size("cols")
    coarse = groups
    count = a_ref.shape[0]
    fine = p_ref.shape[0]
    start = p * fine + g * count
    edge = edge_of(g, p)
    low = g == 0
    columns, slots_of, inner = lookups(pos_ref, cols_ref)

    for f in range(-HB, count + HB):
        x = p_ref[jnp.clip(count * g + f, 0, fine - 1)]
        if f == -HB:
            x = jnp.where(jnp.logical_and(edge, low), jnp.zeros_like(x), x)
        if f == count + HB - 1:
            x = jnp.where(jnp.logical_and(edge, g > 0), jnp.zeros_like(x), x)
        pairs = turned_pairs(x)
        cols = columns(f)
        spread(pairs, slots_of(cols), groups, pd_ref, f + HB)
        if 0 <= f < count:
            spread(pairs, inner(cols), coarse // 2, pn_ref, f)

    zeros = jnp.where(low, 0, count + 2 * HB - 1)
    first = jnp.where(edge, jnp.where(low, 0, count - HB), count)
    for i in range(count):
        later = jnp.logical_and(i >= first, i < first + HB)
        picks = [at_ref[k, g * count + i] - (start - HB) for k in range(KA)]
        picks = [jnp.where(later, zeros, pick) for pick in picks]
        ap_ref[i * B : (i + 1) * B, :] = ap_row(a_ref[i], picks, pd_ref)
    part_ref[...] = transposed_dot(pn_ref[...], ap_ref[...])


def edge_kernel(
    at_ref, pos_ref, cols_ref, steps_ref, own_a_ref, far_a_ref, far_p_ref, pd_ref, pn_ref, part_ref,
    sent_ref, table, lhs, ap_ref,
):
    g, p = lax.axis_index("cols"), lax.axis_index("rows")
    groups = lax.axis_size("cols")
    edge = edge_of(g, p)
    low = g == 0
    size = HB * B
    count = pn_ref.shape[0] // B
    fine = at_ref.shape[1]
    columns, slots_of, inner = lookups(pos_ref, cols_ref)

    def store(total):
        for c in range(groups):
            sent_ref[c] = total[:, c * LANES : (c + 1) * LANES].astype(jnp.bfloat16)

    def half(second):
        return pl.ds(pl.multiple_of(jnp.where(second, size, 0), size), size)

    @pl.when(edge)
    def _():
        rows = pl.ds(pl.multiple_of(jnp.where(low, 2 * size, 0), size), 2 * size)
        table[rows, :] = pd_ref[size : 3 * size, :]
        lhs[half(low), :] = pn_ref[pl.ds(pl.multiple_of(jnp.where(low, 0, (count - HB) * B), B), size), :]
        shift = jnp.where(low, 0, 2 * HB)
        for t in range(2 * HB):
            cols = columns(jnp.where(low, t - 2 * HB, count + t))
            spread(turned_pairs(far_p_ref[t]), slots_of(cols), groups, table, shift + t)
        for t in range(HB):
            s = jnp.where(low, HB, 0) + t
            cols = columns(jnp.where(low, t - HB, count + t))
            row = jnp.where(low, t, HB + t)
            spread(turned_pairs(far_p_ref[s]), inner(cols), groups // 2, lhs, row)
        first = g * count + jnp.where(low, 0, count - HB)
        base = p * fine + g * count - jnp.where(low, 2 * HB, 0)
        for t in range(HB):
            a = own_a_ref[t]
            picks = [at_ref[k, first + t] - base for k in range(KA)]
            ap_ref[block(jnp.where(low, HB + t, t)), :] = ap_row(a, picks, table)
        for t in range(HB):
            a = far_a_ref[t]
            lane = jnp.where(low, fine - HB, 0) + t
            picks = [steps_ref[k, lane] + jnp.where(low, t, HB + t) for k in range(KA)]
            ap_ref[block(jnp.where(low, t, HB + t)), :] = ap_row(a, picks, table)
        store(part_ref[...] + transposed_dot(lhs[...], ap_ref[...]))

    @pl.when(jnp.logical_not(edge))
    def _():
        store(part_ref[...])


def on_device(a_vals, a_cols, p_vals, p_cols, colpos):
    groups = lax.axis_size("cols")
    parts = lax.axis_size("rows")
    count = a_vals.shape[0]
    fine = p_vals.shape[0]
    coarse = groups
    g = lax.axis_index("cols")
    p = lax.axis_index("rows")
    last = groups - 1
    wide = groups * LANES
    bf16, f32 = jnp.bfloat16, jnp.float32
    params = pltpu.CompilerParams(vmem_limit_bytes=16 << 20)
    at = a_cols.T

    far_row = jnp.where(g < groups // 2, fine - 2 * HB, 0)
    longer = jnp.pad(p_vals, ((0, 1), (0, 0), (0, 0)))
    msg_p = lax.dynamic_slice_in_dim(longer, far_row, 2 * HB + 1, 0)
    steps = (at - (p * fine - HB + jnp.arange(fine, dtype=jnp.int32))).astype(bf16)
    steps = jnp.pad(steps[None], ((2 * HB, 0), (0, B - KA), (0, KP * B - fine)))
    row = lax.broadcasted_iota(jnp.int32, msg_p.shape, 0)
    msg_p = jnp.where(row < 2 * HB, msg_p, steps)
    pairs = [(q * groups + 1, (q + 1) * groups) for q in range(parts - 1)]
    pairs += [((q + 1) * groups + last - 1, q * groups + last) for q in range(parts - 1)]
    far_p = lax.ppermute(msg_p, ("rows", "cols"), pairs)
    msg_a = pl.pallas_call(
        pack_kernel,
        out_shape=jax.ShapeDtypeStruct((HB,) + a_vals.shape[1:], bf16),
        in_specs=[VMEM, pl.BlockSpec(memory_space=pl.ANY)],
        out_specs=VMEM,
        compiler_params=params,
        name="pack",
    )(a_vals, msg_p)
    pairs = [(q * groups, (q - 1) * groups + last) for q in range(1, parts)]
    pairs += [(target, source) for source, target in pairs]
    far_a = lax.ppermute(msg_a, ("rows", "cols"), pairs)

    pad = 2 * HB
    padded = jnp.pad(p_cols.T, ((0, 0), (pad, pad)))
    near_cols = lax.dynamic_slice_in_dim(padded, p * fine + g * count, count + 2 * pad, 1)
    pd, pn, part = pl.pallas_call(
        own_kernel,
        out_shape=(
            jax.ShapeDtypeStruct(((count + 2 * HB) * B, wide), bf16),
            jax.ShapeDtypeStruct((count * B, coarse * B), bf16),
            jax.ShapeDtypeStruct((coarse * B, wide), f32),
        ),
        in_specs=[SMEM] * 3 + [VMEM] * 2,
        out_specs=(VMEM, VMEM, VMEM),
        scratch_shapes=[pltpu.VMEM((count * B, wide), bf16)],
        compiler_params=params,
        cost_estimate=pl.CostEstimate(flops=1 << 31, bytes_accessed=4 << 20, transcendentals=0),
        name="own_rows",
    )(at, colpos, near_cols, a_vals, p_vals)

    far_steps = far_p[2 * HB, :KA, :fine].astype(jnp.int32)
    sent = pl.pallas_call(
        edge_kernel,
        out_shape=jax.ShapeDtypeStruct((groups, coarse * B, LANES), bf16),
        in_specs=[SMEM] * 4 + [VMEM] * 6,
        out_specs=VMEM,
        scratch_shapes=[
            pltpu.VMEM((4 * HB * B, wide), bf16),
            pltpu.VMEM((2 * HB * B, coarse * B), bf16),
            pltpu.VMEM((2 * HB * B, wide), bf16),
        ],
        compiler_params=params,
        name="edge_rows",
    )(at, colpos, near_cols, far_steps, msg_a, far_a, far_p, pd, pn, part)

    got = lax.all_to_all(sent, "cols", 0, 0).astype(f32)
    half = groups // 2
    low = sum(got[c] for c in range(1, half)) + got[0]
    high = sum(got[c] for c in range(half + 1, groups)) + got[half]
    out = jnp.pad(low, ((0, 0), (0, B))) + jnp.pad(high, ((0, 0), (B, 0)))
    return out.reshape(coarse, B, 3 * B)


def solution(mesh):
    placed = (P(("rows", "cols"), None, None), P("rows", None), P("rows", None, None), P(), P())
    return jax.shard_map(
        on_device, mesh=mesh, in_specs=placed, out_specs=P("rows", None, "cols"), check_vma=False
    )
```

```python
import jax
import jax.numpy as jnp
from jax import lax
from jax.experimental import pallas as pl
from jax.experimental.pallas import tpu as pltpu
from jax.sharding import PartitionSpec as P

B = 64
KA = 8
KP = 4
HB = 4
LANES = 2 * B
VMEM = pl.BlockSpec(memory_space=pltpu.VMEM)
SMEM = pl.BlockSpec(memory_space=pltpu.SMEM)


def block(i):
    return pl.ds(pl.multiple_of(i * B, B), B)


def edge_of(g, p):
    lower = jnp.logical_and(g == 0, p > 0)
    upper = jnp.logical_and(g == lax.axis_size("cols") - 1, p < lax.axis_size("rows") - 1)
    return jnp.logical_or(lower, upper)


def turned_pairs(x):
    x = x.astype(jnp.float32)
    pairs = [x[:, v * LANES : (v + 1) * LANES] for v in range(KP // 2)]
    return [(pair, pltpu.roll(pair, B, 1)) for pair in pairs]


def spread(pairs, slots, pieces, ref, row):
    left = lax.broadcasted_iota(jnp.int32, (1, LANES), 1) < B
    side = jnp.where(left, 0, 1)
    keeps = [jnp.where(left, slots[2 * v], slots[2 * v + 1]) - side for v in range(len(pairs))]
    swaps = [jnp.where(left, slots[2 * v + 1], slots[2 * v]) - side for v in range(len(pairs))]
    for c in range(pieces):
        total = jnp.zeros((B, LANES), jnp.float32)
        for (pair, turned), keep, swap in zip(pairs, keeps, swaps):
            total = jnp.where(keep == 2 * c, pair, jnp.where(swap == 2 * c, turned, total))
        ref[block(row), c * LANES : (c + 1) * LANES] = total.astype(jnp.bfloat16)


def ap_row(a, indices, pd_ref):
    picked = jnp.concatenate([pd_ref[block(i), :] for i in indices], axis=0)
    return jnp.dot(a, picked, preferred_element_type=jnp.float32).astype(jnp.bfloat16)


def transposed_dot(x, y):
    return lax.dot_general(x, y, (((0,), (0,)), ((), ())), preferred_element_type=jnp.float32)


def pack_kernel(a_ref, _, msg_ref):
    first = jnp.where(lax.axis_index("cols") == 0, 0, a_ref.shape[0] - HB)
    msg_ref[...] = a_ref[pl.ds(first, HB)]


def lookups(pos_ref, cols_ref):
    g, p = lax.axis_index("cols"), lax.axis_index("rows")
    coarse = groups = lax.axis_size("cols")
    base = 1 - p - jnp.where(g < groups // 2, 0, 1)

    def columns(f):
        return [cols_ref[m, f + 2 * HB] for m in range(KP)]

    def slots_of(cols):
        return [2 * pos_ref[h] + lax.div(h, coarse) + base for h in cols]

    def inner(cols):
        return [h - p * coarse for h in cols]

    return columns, slots_of, inner


def own_kernel(at_ref, pos_ref, cols_ref, a_ref, p_ref, pd_ref, pn_ref, part_ref, ap_ref):
    g, p = lax.axis_index("cols"), lax.axis_index("rows")
    groups = lax.axis_size("cols")
    coarse = groups
    count = a_ref.shape[0]
    fine = p_ref.shape[0]
    start = p * fine + g * count
    edge = edge_of(g, p)
    low = g == 0
    columns, slots_of, inner = lookups(pos_ref, cols_ref)

    for f in range(-HB, count + HB):
        x = p_ref[jnp.clip(count * g + f, 0, fine - 1)]
        if f == -HB:
            x = jnp.where(jnp.logical_and(edge, low), jnp.zeros_like(x), x)
        if f == count + HB - 1:
            x = jnp.where(jnp.logical_and(edge, g > 0), jnp.zeros_like(x), x)
        pairs = turned_pairs(x)
        cols = columns(f)
        spread(pairs, slots_of(cols), groups, pd_ref, f + HB)
        if 0 <= f < count:
            spread(pairs, inner(cols), coarse // 2, pn_ref, f)

    zeros = jnp.where(low, 0, count + 2 * HB - 1)
    first = jnp.where(edge, jnp.where(low, 0, count - HB), count)
    for i in range(count):
        later = jnp.logical_and(i >= first, i < first + HB)
        picks = [at_ref[k, g * count + i] - (start - HB) for k in range(KA)]
        picks = [jnp.where(later, zeros, pick) for pick in picks]
        ap_ref[i * B : (i + 1) * B, :] = ap_row(a_ref[i], picks, pd_ref)
    part_ref[...] = transposed_dot(pn_ref[...], ap_ref[...])


def halo_kernel(
    at_ref, pos_ref, cols_ref, own_a_ref, far_p_ref, pd_ref, pn_ref, table, lhs, more_ref, ap_ref
):
    g, p = lax.axis_index("cols"), lax.axis_index("rows")
    groups = lax.axis_size("cols")
    low = g == 0
    size = HB * B
    count = pn_ref.shape[0] // B
    fine = at_ref.shape[1]
    columns, slots_of, inner = lookups(pos_ref, cols_ref)

    @pl.when(edge_of(g, p))
    def _():
        rows = pl.ds(pl.multiple_of(jnp.where(low, 2 * size, 0), size), 2 * size)
        table[rows, :] = pd_ref[size : 3 * size, :]
        shift = jnp.where(low, 0, 2 * HB)
        for t in range(2 * HB):
            cols = columns(jnp.where(low, t - 2 * HB, count + t))
            spread(turned_pairs(far_p_ref[t]), slots_of(cols), groups, table, shift + t)
        for t in range(HB):
            cols = columns(jnp.where(low, t - HB, count + t))
            row = turned_pairs(far_p_ref[jnp.where(low, HB, 0) + t])
            spread(row, inner(cols), groups // 2, lhs, t)
        first = jnp.where(low, 0, count - HB)
        base = p * fine + g * count - jnp.where(low, 2 * HB, 0)
        for t in range(HB):
            picks = [at_ref[k, g * count + first + t] - base for k in range(KA)]
            ap_ref[t * B : (t + 1) * B, :] = ap_row(own_a_ref[t], picks, table)
        own = pn_ref[pl.ds(pl.multiple_of(first * B, B), size), :]
        more_ref[...] = transposed_dot(own, ap_ref[...])


def edge_kernel(steps_ref, far_a_ref, table, lhs, part_ref, more_ref, sent_ref, ap_ref):
    g, p = lax.axis_index("cols"), lax.axis_index("rows")
    groups = lax.axis_size("cols")
    edge = edge_of(g, p)
    low = g == 0
    fine = steps_ref.shape[1]

    def store(total):
        for c in range(groups):
            sent_ref[c] = total[:, c * LANES : (c + 1) * LANES].astype(jnp.bfloat16)

    @pl.when(edge)
    def _():
        for t in range(HB):
            lane = jnp.where(low, fine - HB, 0) + t
            picks = [steps_ref[k, lane] + jnp.where(low, t, HB + t) for k in range(KA)]
            ap_ref[t * B : (t + 1) * B, :] = ap_row(far_a_ref[t], picks, table)
        store(part_ref[...] + more_ref[...] + transposed_dot(lhs[...], ap_ref[...]))

    @pl.when(jnp.logical_not(edge))
    def _():
        store(part_ref[...])


def on_device(a_vals, a_cols, p_vals, p_cols, colpos):
    groups = lax.axis_size("cols")
    parts = lax.axis_size("rows")
    count = a_vals.shape[0]
    fine = p_vals.shape[0]
    coarse = groups
    g = lax.axis_index("cols")
    p = lax.axis_index("rows")
    last = groups - 1
    wide = groups * LANES
    bf16, f32 = jnp.bfloat16, jnp.float32
    params = pltpu.CompilerParams(vmem_limit_bytes=16 << 20)
    at = a_cols.T

    far_row = jnp.where(g < groups // 2, fine - 2 * HB, 0)
    longer = jnp.pad(p_vals, ((0, 1), (0, 0), (0, 0)))
    msg_p = lax.dynamic_slice_in_dim(longer, far_row, 2 * HB + 1, 0)
    steps = (at - (p * fine - HB + jnp.arange(fine, dtype=jnp.int32))).astype(bf16)
    steps = jnp.pad(steps[None], ((2 * HB, 0), (0, B - KA), (0, KP * B - fine)))
    row = lax.broadcasted_iota(jnp.int32, msg_p.shape, 0)
    msg_p = jnp.where(row < 2 * HB, msg_p, steps)
    pairs = [(q * groups + 1, (q + 1) * groups) for q in range(parts - 1)]
    pairs += [((q + 1) * groups + last - 1, q * groups + last) for q in range(parts - 1)]
    far_p = lax.ppermute(msg_p, ("rows", "cols"), pairs)
    msg_a = pl.pallas_call(
        pack_kernel,
        out_shape=jax.ShapeDtypeStruct((HB,) + a_vals.shape[1:], bf16),
        in_specs=[VMEM, pl.BlockSpec(memory_space=pl.ANY)],
        out_specs=VMEM,
        compiler_params=params,
        name="pack",
    )(a_vals, msg_p)
    pairs = [(q * groups, (q - 1) * groups + last) for q in range(1, parts)]
    pairs += [(target, source) for source, target in pairs]
    far_a = lax.ppermute(msg_a, ("rows", "cols"), pairs)

    pad = 2 * HB
    padded = jnp.pad(p_cols.T, ((0, 0), (pad, pad)))
    near_cols = lax.dynamic_slice_in_dim(padded, p * fine + g * count, count + 2 * pad, 1)
    pd, pn, part = pl.pallas_call(
        own_kernel,
        out_shape=(
            jax.ShapeDtypeStruct(((count + 2 * HB) * B, wide), bf16),
            jax.ShapeDtypeStruct((count * B, coarse * B), bf16),
            jax.ShapeDtypeStruct((coarse * B, wide), f32),
        ),
        in_specs=[SMEM] * 3 + [VMEM] * 2,
        out_specs=(VMEM, VMEM, VMEM),
        scratch_shapes=[pltpu.VMEM((count * B, wide), bf16)],
        compiler_params=params,
        cost_estimate=pl.CostEstimate(flops=1 << 31, bytes_accessed=4 << 20, transcendentals=0),
        name="own_rows",
    )(at, colpos, near_cols, a_vals, p_vals)

    table, far_pn, more = pl.pallas_call(
        halo_kernel,
        out_shape=(
            jax.ShapeDtypeStruct((4 * HB * B, wide), bf16),
            jax.ShapeDtypeStruct((HB * B, coarse * B), bf16),
            jax.ShapeDtypeStruct((coarse * B, wide), f32),
        ),
        in_specs=[SMEM] * 3 + [VMEM] * 4,
        out_specs=(VMEM, VMEM, VMEM),
        scratch_shapes=[pltpu.VMEM((HB * B, wide), bf16)],
        compiler_params=params,
        cost_estimate=pl.CostEstimate(flops=1 << 30, bytes_accessed=2 << 20, transcendentals=0),
        name="halo_rows",
    )(at, colpos, near_cols, msg_a, far_p, pd, pn)

    far_steps = far_p[2 * HB, :KA, :fine].astype(jnp.int32)
    sent = pl.pallas_call(
        edge_kernel,
        out_shape=jax.ShapeDtypeStruct((groups, coarse * B, LANES), bf16),
        in_specs=[SMEM] + [VMEM] * 5,
        out_specs=VMEM,
        scratch_shapes=[pltpu.VMEM((HB * B, wide), bf16)],
        compiler_params=params,
        name="edge_rows",
    )(far_steps, far_a, table, far_pn, part, more)

    got = lax.all_to_all(sent, "cols", 0, 0).astype(f32)
    half = groups // 2
    low = sum(got[c] for c in range(1, half)) + got[0]
    high = sum(got[c] for c in range(half + 1, groups)) + got[half]
    out = jnp.pad(low, ((0, 0), (0, B))) + jnp.pad(high, ((0, 0), (B, 0)))
    return out.reshape(coarse, B, 3 * B)


def solution(mesh):
    placed = (P(("rows", "cols"), None, None), P("rows", None), P("rows", None, None), P(), P())
    return jax.shard_map(
        on_device, mesh=mesh, in_specs=placed, out_specs=P("rows", None, "cols"), check_vma=False
    )
```

```python
import jax
import jax.numpy as jnp
from jax import lax
from jax.experimental import pallas as pl
from jax.experimental.pallas import tpu as pltpu
from jax.sharding import PartitionSpec as P

B = 64
KA = 8
KP = 4
HB = 4
LANES = 2 * B
VMEM = pl.BlockSpec(memory_space=pltpu.VMEM)
SMEM = pl.BlockSpec(memory_space=pltpu.SMEM)
ANY = pl.BlockSpec(memory_space=pl.ANY)


def block(i):
    return pl.ds(pl.multiple_of(i * B, B), B)


def edge_of(g, p):
    lower = jnp.logical_and(g == 0, p > 0)
    upper = jnp.logical_and(g == lax.axis_size("cols") - 1, p < lax.axis_size("rows") - 1)
    return jnp.logical_or(lower, upper)


def turned_pairs(x):
    x = x.astype(jnp.float32)
    pairs = [x[:, v * LANES : (v + 1) * LANES] for v in range(KP // 2)]
    return [(pair, pltpu.roll(pair, B, 1)) for pair in pairs]


def spread(pairs, slots, pieces, ref, row):
    left = lax.broadcasted_iota(jnp.int32, (1, LANES), 1) < B
    side = jnp.where(left, 0, 1)
    keeps = [jnp.where(left, slots[2 * v], slots[2 * v + 1]) - side for v in range(len(pairs))]
    swaps = [jnp.where(left, slots[2 * v + 1], slots[2 * v]) - side for v in range(len(pairs))]
    for c in range(pieces):
        total = jnp.zeros((B, LANES), jnp.float32)
        for (pair, turned), keep, swap in zip(pairs, keeps, swaps):
            total = jnp.where(keep == 2 * c, pair, jnp.where(swap == 2 * c, turned, total))
        ref[block(row), c * LANES : (c + 1) * LANES] = total.astype(jnp.bfloat16)


def ap_row(a, indices, pd_ref):
    picked = jnp.concatenate([pd_ref[block(i), :] for i in indices], axis=0)
    return jnp.dot(a, picked, preferred_element_type=jnp.float32).astype(jnp.bfloat16)


def transposed_dot(x, y):
    return lax.dot_general(x, y, (((0,), (0,)), ((), ())), preferred_element_type=jnp.float32)


def pack_kernel(a_ref, _, msg_ref):
    first = jnp.where(lax.axis_index("cols") == 0, 0, a_ref.shape[0] - HB)
    msg_ref[...] = a_ref[pl.ds(first, HB)]


def lookups(pos_ref, cols_ref):
    g, p = lax.axis_index("cols"), lax.axis_index("rows")
    coarse = groups = lax.axis_size("cols")
    base = 1 - p - jnp.where(g < groups // 2, 0, 1)

    def columns(f):
        return [cols_ref[m, f + 2 * HB] for m in range(KP)]

    def slots_of(cols):
        return [2 * pos_ref[h] + lax.div(h, coarse) + base for h in cols]

    def inner(cols):
        return [h - p * coarse for h in cols]

    return columns, slots_of, inner


def own_kernel(at_ref, pos_ref, cols_ref, a_ref, p_ref, pd_ref, pn_ref, part_ref, ap_ref):
    g, p = lax.axis_index("cols"), lax.axis_index("rows")
    groups = lax.axis_size("cols")
    coarse = groups
    count = a_ref.shape[0]
    fine = p_ref.shape[0]
    start = p * fine + g * count
    edge = edge_of(g, p)
    low = g == 0
    columns, slots_of, inner = lookups(pos_ref, cols_ref)

    for f in range(-HB, count + HB):
        x = p_ref[jnp.clip(count * g + f, 0, fine - 1)]
        if f == -HB:
            x = jnp.where(jnp.logical_and(edge, low), jnp.zeros_like(x), x)
        if f == count + HB - 1:
            x = jnp.where(jnp.logical_and(edge, g > 0), jnp.zeros_like(x), x)
        pairs = turned_pairs(x)
        cols = columns(f)
        spread(pairs, slots_of(cols), groups, pd_ref, f + HB)
        if 0 <= f < count:
            spread(pairs, inner(cols), coarse // 2, pn_ref, f)

    zeros = jnp.where(low, 0, count + 2 * HB - 1)
    first = jnp.where(edge, jnp.where(low, 0, count - HB), count)
    for i in range(count):
        later = jnp.logical_and(i >= first, i < first + HB)
        picks = [at_ref[k, g * count + i] - (start - HB) for k in range(KA)]
        picks = [jnp.where(later, zeros, pick) for pick in picks]
        ap_ref[i * B : (i + 1) * B, :] = ap_row(a_ref[i], picks, pd_ref)
    part_ref[...] = transposed_dot(pn_ref[...], ap_ref[...])


def halo_kernel(
    at_hbm, pos_hbm, cols_hbm, own_a_ref, far_p_ref, pd_ref, pn_ref,
    table, lhs, more_ref,
    ap_ref, at_ref, pos_ref, cols_ref, sems,
):
    g, p = lax.axis_index("cols"), lax.axis_index("rows")
    groups = lax.axis_size("cols")
    low = g == 0
    size = HB * B
    count = pn_ref.shape[0] // B
    fine = at_ref.shape[1]
    columns, slots_of, inner = lookups(pos_ref, cols_ref)

    @pl.when(edge_of(g, p))
    def _():
        pairs = [(at_hbm, at_ref), (pos_hbm, pos_ref), (cols_hbm, cols_ref)]
        copies = [pltpu.make_async_copy(x, y, sems.at[n]) for n, (x, y) in enumerate(pairs)]
        for copy in copies:
            copy.start()
        rows = pl.ds(pl.multiple_of(jnp.where(low, 2 * size, 0), size), 2 * size)
        table[rows, :] = pd_ref[size : 3 * size, :]
        for copy in copies:
            copy.wait()
        shift = jnp.where(low, 0, 2 * HB)
        for t in range(2 * HB):
            cols = columns(jnp.where(low, t - 2 * HB, count + t))
            spread(turned_pairs(far_p_ref[t]), slots_of(cols), groups, table, shift + t)
        for t in range(HB):
            cols = columns(jnp.where(low, t - HB, count + t))
            row = turned_pairs(far_p_ref[jnp.where(low, HB, 0) + t])
            spread(row, inner(cols), groups // 2, lhs, t)
        first = jnp.where(low, 0, count - HB)
        base = p * fine + g * count - jnp.where(low, 2 * HB, 0)
        for t in range(HB):
            picks = [at_ref[k, g * count + first + t] - base for k in range(KA)]
            ap_ref[t * B : (t + 1) * B, :] = ap_row(own_a_ref[t], picks, table)
        own = pn_ref[pl.ds(pl.multiple_of(first * B, B), size), :]
        more_ref[...] = transposed_dot(own, ap_ref[...])


def edge_kernel(
    steps_hbm, far_a_ref, table, lhs, part_ref, more_ref, sent_ref, ap_ref, steps_ref, sem
):
    g, p = lax.axis_index("cols"), lax.axis_index("rows")
    groups = lax.axis_size("cols")
    edge = edge_of(g, p)
    low = g == 0
    fine = steps_ref.shape[1]

    def store(total):
        for c in range(groups):
            sent_ref[c] = total[:, c * LANES : (c + 1) * LANES].astype(jnp.bfloat16)

    @pl.when(edge)
    def _():
        copy = pltpu.make_async_copy(steps_hbm, steps_ref, sem)
        copy.start()
        copy.wait()
        for t in range(HB):
            lane = jnp.where(low, fine - HB, 0) + t
            picks = [steps_ref[k, lane] + jnp.where(low, t, HB + t) for k in range(KA)]
            ap_ref[t * B : (t + 1) * B, :] = ap_row(far_a_ref[t], picks, table)
        store(part_ref[...] + more_ref[...] + transposed_dot(lhs[...], ap_ref[...]))

    @pl.when(jnp.logical_not(edge))
    def _():
        store(part_ref[...])


def on_device(a_vals, a_cols, p_vals, p_cols, colpos):
    groups = lax.axis_size("cols")
    parts = lax.axis_size("rows")
    count = a_vals.shape[0]
    fine = p_vals.shape[0]
    coarse = groups
    g = lax.axis_index("cols")
    p = lax.axis_index("rows")
    last = groups - 1
    wide = groups * LANES
    bf16, f32 = jnp.bfloat16, jnp.float32
    params = pltpu.CompilerParams(vmem_limit_bytes=16 << 20)
    at = a_cols.T

    far_row = jnp.where(g < groups // 2, fine - 2 * HB, 0)
    longer = jnp.pad(p_vals, ((0, 1), (0, 0), (0, 0)))
    msg_p = lax.dynamic_slice_in_dim(longer, far_row, 2 * HB + 1, 0)
    steps = (at - (p * fine - HB + jnp.arange(fine, dtype=jnp.int32))).astype(bf16)
    steps = jnp.pad(steps[None], ((2 * HB, 0), (0, B - KA), (0, KP * B - fine)))
    row = lax.broadcasted_iota(jnp.int32, msg_p.shape, 0)
    msg_p = jnp.where(row < 2 * HB, msg_p, steps)
    pairs = [(q * groups + 1, (q + 1) * groups) for q in range(parts - 1)]
    pairs += [((q + 1) * groups + last - 1, q * groups + last) for q in range(parts - 1)]
    far_p = lax.ppermute(msg_p, ("rows", "cols"), pairs)
    msg_a = pl.pallas_call(
        pack_kernel,
        out_shape=jax.ShapeDtypeStruct((HB,) + a_vals.shape[1:], bf16),
        in_specs=[VMEM, pl.BlockSpec(memory_space=pl.ANY)],
        out_specs=VMEM,
        compiler_params=params,
        name="pack",
    )(a_vals, msg_p)
    pairs = [(q * groups, (q - 1) * groups + last) for q in range(1, parts)]
    pairs += [(target, source) for source, target in pairs]
    far_a = lax.ppermute(msg_a, ("rows", "cols"), pairs)

    pad = 2 * HB
    padded = jnp.pad(p_cols.T, ((0, 0), (pad, pad)))
    near_cols = lax.dynamic_slice_in_dim(padded, p * fine + g * count, count + 2 * pad, 1)
    pd, pn, part = pl.pallas_call(
        own_kernel,
        out_shape=(
            jax.ShapeDtypeStruct(((count + 2 * HB) * B, wide), bf16),
            jax.ShapeDtypeStruct((count * B, coarse * B), bf16),
            jax.ShapeDtypeStruct((coarse * B, wide), f32),
        ),
        in_specs=[SMEM] * 3 + [VMEM] * 2,
        out_specs=(VMEM, VMEM, VMEM),
        scratch_shapes=[pltpu.VMEM((count * B, wide), bf16)],
        compiler_params=params,
        cost_estimate=pl.CostEstimate(flops=1 << 31, bytes_accessed=4 << 20, transcendentals=0),
        name="own_rows",
    )(at, colpos, near_cols, a_vals, p_vals)

    table, far_pn, more = pl.pallas_call(
        halo_kernel,
        out_shape=(
            jax.ShapeDtypeStruct((4 * HB * B, wide), bf16),
            jax.ShapeDtypeStruct((HB * B, coarse * B), bf16),
            jax.ShapeDtypeStruct((coarse * B, wide), f32),
        ),
        in_specs=[ANY] * 3 + [VMEM] * 4,
        out_specs=(VMEM, VMEM, VMEM),
        scratch_shapes=[
            pltpu.VMEM((HB * B, wide), bf16),
            pltpu.SMEM(at.shape, jnp.int32),
            pltpu.SMEM(colpos.shape, jnp.int32),
            pltpu.SMEM(near_cols.shape, jnp.int32),
            pltpu.SemaphoreType.DMA((3,)),
        ],
        compiler_params=params,
        cost_estimate=pl.CostEstimate(flops=1 << 30, bytes_accessed=2 << 20, transcendentals=0),
        name="halo_rows",
    )(at, colpos, near_cols, msg_a, far_p, pd, pn)

    far_steps = far_p[2 * HB, :KA, :fine].astype(jnp.int32)
    sent = pl.pallas_call(
        edge_kernel,
        out_shape=jax.ShapeDtypeStruct((groups, coarse * B, LANES), bf16),
        in_specs=[ANY] + [VMEM] * 5,
        out_specs=VMEM,
        scratch_shapes=[
            pltpu.VMEM((HB * B, wide), bf16),
            pltpu.SMEM(at.shape, jnp.int32),
            pltpu.SemaphoreType.DMA,
        ],
        compiler_params=params,
        name="edge_rows",
    )(far_steps, far_a, table, far_pn, part, more)

    got = lax.all_to_all(sent, "cols", 0, 0).astype(f32)
    half = groups // 2
    low = sum(got[c] for c in range(1, half)) + got[0]
    high = sum(got[c] for c in range(half + 1, groups)) + got[half]
    out = jnp.pad(low, ((0, 0), (0, B))) + jnp.pad(high, ((0, 0), (B, 0)))
    return out.reshape(coarse, B, 3 * B)


def solution(mesh):
    placed = (P(("rows", "cols"), None, None), P("rows", None), P("rows", None, None), P(), P())
    return jax.shard_map(
        on_device, mesh=mesh, in_specs=placed, out_specs=P("rows", None, "cols"), check_vma=False
    )
```
